32 devices in a mesh: mic: 8 (over z, y), mode: 4 (over x, core).
Axes of the slice: x: 2, y: 2, z: 4, core: 2. Of those that a mesh axis runs over, the one named last changes fastest.
Arguments:
- signal: bfloat16 [8, 2048, 4096], P('mic', 'mode'), may hold values from -6 to 6
- mic_axial: int32 [2048], P('mic'), may hold values from 0 to 63
- mic_azimuth: int32 [2048], P('mic'), may hold values from 0 to 511
- mode_m: int32 [8192], P('mode'), may hold values from -128 to 127
- mode_n: int32 [8192], P('mode'), may hold values from 0 to 31
- freq_bins: int32 [16], replicated, may hold values from 1 to 1023
Outputs:
- amplitude: float32 [16, 2, 8, 8192], P(None, None, None, 'mode')
- power: float32 [16, 8192], P(None, 'mode')
- residual: float32 [16, 2, 8, 2048], P('mode', None, None, 'mic')
The draws below stay inside these ranges and needn't reach their ends.
All inputs are finite; a program needn't handle non-finite values.
Results may differ from the reference program's by a relative error of at most 0.0051.
Values may be sent and summed in bfloat16 or wider, within the bound.
A program may use at most 64 MiB of HBM per device.

```python
import math
import jax
import jax.numpy as jnp
from jax import lax

SEGLEN = 4096
FREQS = 16
MODES = 8192
ITERS = 2
AZIM = 512
AXIAL = 64
NRAD = 32
MICS = 2048
SEGS = 8


def plant(result, stream_key, smallest, largest):
    place = [jax.random.randint(jax.random.fold_in(stream_key, axis), (), 0, length) for axis, length in enumerate(result.shape)]
    main_axis = result.shape.index(max(result.shape))
    beside = place[:main_axis] + [(place[main_axis] + 1) % result.shape[main_axis]] + place[main_axis + 1:]
    return result.at[tuple(place)].set(smallest).at[tuple(beside)].set(largest)


def block_scale(rng, shape, pieces, low, high):
    def one(axis_at, parts):
        steps = jax.random.uniform(jax.random.fold_in(jax.random.fold_in(rng, 6), axis_at), (parts,), jnp.float32, low / len(pieces), high / len(pieces))
        return jnp.repeat(jnp.exp(steps), shape[axis_at] // parts).reshape((-1,) + (1,) * (len(shape) - axis_at - 1))

    loudness = one(*pieces[0])
    for cut in pieces[1:]:
        loudness = loudness * one(*cut)
    return loudness


def bell_draw(key, dims, spread, bound, pieces=(), kind=jnp.bfloat16):
    factor_of = block_scale(key, dims, pieces, -0.22, 0.18) if pieces else 1.0
    values = jax.random.normal(key, dims, jnp.float32) * spread * factor_of
    return jnp.minimum(jnp.maximum(values, -bound), bound).astype(kind)


def setup_inputs(seed: int = 0) -> dict:
    seeds = jax.random.split(jax.random.key(seed), 7)
    signal = bell_draw(seeds[0], (SEGS, MICS, SEGLEN), 1.0, 6.0, ((0, 8), (1, 4)))
    mic_axial = plant(jax.random.randint(seeds[1], (MICS,), 0, AXIAL), jax.random.fold_in(seeds[1], 1), 0, AXIAL - 1).astype(jnp.int32)
    mic_azimuth = plant(jax.random.randint(seeds[2], (MICS,), 0, AZIM), jax.random.fold_in(seeds[2], 1), 0, AZIM - 1).astype(jnp.int32)
    mode_m = plant(jax.random.randint(seeds[3], (MODES,), -128, 128), jax.random.fold_in(seeds[3], 1), -128, 127).astype(jnp.int32)
    mode_n = plant(jax.random.randint(seeds[4], (MODES,), 0, NRAD), jax.random.fold_in(seeds[4], 1), 0, NRAD - 1).astype(jnp.int32)
    freq_bins = plant(jax.random.randint(seeds[5], (FREQS,), 1, SEGLEN // 4), jax.random.fold_in(seeds[5], 1), 1, (SEGLEN // 4) - 1).astype(jnp.int32)
    return dict(signal=signal, mic_axial=mic_axial, mic_azimuth=mic_azimuth, mode_m=mode_m, mode_n=mode_n, freq_bins=freq_bins)


EPS = 1e-06

def analysis_rows(freq_bins, seglen):
    sample_index = jnp.arange(seglen, dtype=jnp.int32)
    phase_turns = jnp.mod(freq_bins[:, None] * sample_index[None, :], seglen)
    phase_angle = phase_turns.astype(jnp.float32) * (2.0 * math.pi / seglen)
    window = 0.5 - 0.5 * jnp.cos(sample_index.astype(jnp.float32) * (2.0 * math.pi / seglen))
    norm_scale = (3.0 * seglen / 8.0) ** (-0.5)
    cosine = window[None, :] * jnp.cos(phase_angle) * norm_scale
    sine = -window[None, :] * jnp.sin(phase_angle) * norm_scale
    stacked = jnp.stack([cosine, sine], axis=1)
    return stacked.reshape(2 * freq_bins.shape[0], seglen).astype(jnp.bfloat16)

def mode_tile(bin_value, mic_axial, mic_azimuth, mode_m, mode_n, norm_scale):
    period = AZIM * AXIAL
    phase_turns = jnp.mod(mic_azimuth[:, None] * (mode_m * AXIAL)[None, :] + mic_axial[:, None] * (bin_value * (2 * NRAD - mode_n))[None, :], period)
    phase_angle = phase_turns.astype(jnp.float32) * (2.0 * math.pi / period)
    weight = norm_scale / jnp.sqrt(1.0 + mode_n.astype(jnp.float32))
    real_part = (weight[None, :] * jnp.cos(phase_angle)).astype(jnp.bfloat16)
    imag_part = (weight[None, :] * jnp.sin(phase_angle)).astype(jnp.bfloat16)
    return (real_part, imag_part)

def forward_product(real_part, imag_part, vector):
    segs = vector.shape[1]
    stacked = vector.reshape(2 * segs, vector.shape[2]).astype(jnp.bfloat16)
    first = jnp.dot(stacked, real_part.T, preferred_element_type=jnp.float32)
    second = jnp.dot(stacked, imag_part.T, preferred_element_type=jnp.float32)
    return jnp.stack([first[:segs] - second[segs:], first[segs:] + second[:segs]])

def adjoint_product(real_part, imag_part, vector):
    segs = vector.shape[1]
    stacked = vector.reshape(2 * segs, vector.shape[2]).astype(jnp.bfloat16)
    first = jnp.dot(stacked, real_part, preferred_element_type=jnp.float32)
    second = jnp.dot(stacked, imag_part, preferred_element_type=jnp.float32)
    return jnp.stack([first[:segs] + second[segs:], first[segs:] - second[:segs]])

def reference(signal, mic_axial, mic_azimuth, mode_m, mode_n, freq_bins):
    analysis = analysis_rows(freq_bins, SEGLEN)

    def transform(segment):
        return jnp.dot(analysis, segment.T, preferred_element_type=jnp.float32)
    spectra = lax.map(transform, signal)
    rhs = spectra.reshape(SEGS, FREQS, 2, MICS).transpose(1, 2, 0, 3)
    norm_scale = MICS ** (-0.5)

    def solve(item):
        bin_value, right_side = item
        real_part, imag_part = mode_tile(bin_value, mic_axial, mic_azimuth, mode_m, mode_n, norm_scale)
        residual = right_side
        gradient = adjoint_product(real_part, imag_part, residual)
        grad_norm = lax.optimization_barrier(jnp.sum(gradient * gradient, axis=(0, 2)))
        direction = gradient
        amplitude = jnp.zeros_like(direction)
        for sweep in range(ITERS):
            image = forward_product(real_part, imag_part, direction)
            image_norm = lax.optimization_barrier(jnp.sum(image * image, axis=(0, 2)))
            step_size = grad_norm / (image_norm + EPS)
            amplitude = amplitude + step_size[None, :, None] * direction
            residual = residual - step_size[None, :, None] * image
            if sweep + 1 < ITERS:
                gradient = adjoint_product(real_part, imag_part, residual)
                next_norm = lax.optimization_barrier(jnp.sum(gradient * gradient, axis=(0, 2)))
                direction = gradient + (next_norm / (grad_norm + EPS))[None, :, None] * direction
                grad_norm = next_norm
        return (amplitude, residual)
    amplitude, residual = lax.map(solve, (freq_bins, rhs))
    power = lax.optimization_barrier(jnp.mean(lax.optimization_barrier(jnp.sum(amplitude * amplitude, axis=1)), axis=1))
    return (amplitude, power, residual)
```

```python
import functools
import math

import jax
import jax.numpy as jnp
from jax import lax
from jax.experimental import pallas as pl
from jax.experimental.pallas import tpu as pltpu
from jax.sharding import PartitionSpec as P

AZIM = 512
AXIAL = 64
NRAD = 32
ORDERS = 256
EPS = 1e-06
NT = (((1,), (1,)), ((), ()))
NN = (((1,), (0,)), ((), ()))


def cos_sin(turns, period):
    quarter = period // 4
    shifted = turns + quarter // 2
    quadrant = lax.shift_right_arithmetic(
        shifted, jnp.int32(quarter.bit_length() - 1)
    )
    rest = jnp.bitwise_and(shifted, quarter - 1) - quarter // 2
    x = rest.astype(jnp.float32) * (2.0 * math.pi / period)
    x2 = x * x
    c = 1.0 + x2 * (-0.5 + x2 * (1.0 / 24 + x2 * (-1.0 / 720 + x2 * (1.0 / 40320))))
    s = x * (1.0 + x2 * (-1.0 / 6 + x2 * (1.0 / 120 + x2 * (-1.0 / 5040 + x2 * (1.0 / 362880)))))
    odd = jnp.bitwise_and(quadrant, 1) == 1
    cos_flip = jnp.bitwise_and(quadrant + 1, 2) == 2
    sin_flip = jnp.bitwise_and(quadrant, 2) == 2
    cos_val = jnp.where(odd, s, c)
    sin_val = jnp.where(odd, c, s)
    return jnp.where(cos_flip, -cos_val, cos_val), jnp.where(sin_flip, -sin_val, sin_val)


def analysis_rows(freq_bins, seglen):
    sample_index = jnp.arange(seglen, dtype=jnp.int32)
    cosine, sine = cos_sin(freq_bins[:, None] * sample_index[None, :], seglen)
    wave, _ = cos_sin(sample_index, seglen)
    window = (0.5 - 0.5 * wave) * (3.0 * seglen / 8.0) ** (-0.5)
    stacked = jnp.stack([window[None, :] * cosine, -window[None, :] * sine], axis=1)
    return stacked.reshape(2 * freq_bins.shape[0], seglen).astype(jnp.bfloat16)


def solve_kernel(
    pairs, segs, chunk, bins_ref, az_ref, ax_ref, m_ref, n_ref, rhs_ref, amp_ref, res_ref,
    t_re, t_im, g_re, g_im, image_ref, hot_ref,
):
    mics = rhs_ref.shape[1]
    modes = m_ref.shape[1]
    half = pairs * NRAD
    scale = 1.0 / mics
    chunks = [pl.ds(at, chunk) for at in range(0, mics, chunk)]
    mode_chunks = [pl.ds(at, chunk) for at in range(0, modes, chunk)]

    orders = lax.broadcasted_iota(jnp.int32, (ORDERS, chunk), 0) - ORDERS // 2
    radial = lax.broadcasted_iota(jnp.int32, (NRAD, chunk), 0)
    for part in chunks:
        cosine, sine = cos_sin(orders * az_ref[:, part], AZIM)
        g_re[:, part] = cosine.astype(jnp.bfloat16)
        g_im[:, part] = sine.astype(jnp.bfloat16)
        for f in range(pairs // segs):
            cosine, sine = cos_sin(ax_ref[:, part] * ((2 * NRAD - radial) * bins_ref[f]), AZIM * AXIAL)
            for s in range(segs):
                rows = pl.ds((f * segs + s) * NRAD, NRAD)
                t_re[rows, part] = cosine
                t_im[rows, part] = sine
    count = jnp.zeros((NRAD, ORDERS), jnp.float32)
    for part in mode_chunks:
        hot = jnp.where(orders == m_ref[:, part], 1.0, 0.0).astype(jnp.bfloat16)
        hot_ref[:, part] = hot
        radial_hot = jnp.where(radial == n_ref[:, part], 1.0, 0.0).astype(jnp.bfloat16)
        count += lax.dot_general(radial_hot, hot, NT, preferred_element_type=jnp.float32)
    radial_col = lax.broadcasted_iota(jnp.int32, (NRAD, ORDERS), 0).astype(jnp.float32)
    gram = count * (scale / (1.0 + radial_col))
    gram = jnp.concatenate([gram] * pairs, axis=0)

    def adjoint(source):
        cos_sum = jnp.zeros((2 * half, ORDERS), jnp.float32)
        sin_sum = jnp.zeros((2 * half, ORDERS), jnp.float32)
        for part in chunks:
            re_rows, im_rows = [], []
            for p in range(pairs):
                rows = pl.ds(p * NRAD, NRAD)
                a, b = t_re[rows, part], t_im[rows, part]
                v, w = source[p : p + 1, part], source[pairs + p : pairs + p + 1, part]
                re_rows.append((a * v + b * w).astype(jnp.bfloat16))
                im_rows.append((a * w - b * v).astype(jnp.bfloat16))
            x = jnp.concatenate(re_rows + im_rows, axis=0)
            cos_sum += lax.dot_general(x, g_re[:, part], NT, preferred_element_type=jnp.float32)
            sin_sum += lax.dot_general(x, g_im[:, part], NT, preferred_element_type=jnp.float32)
        return cos_sum[:half] + sin_sum[half:], cos_sum[half:] - sin_sum[:half]

    def forward(grid_re, grid_im):
        h = jnp.concatenate([gram * grid_re, gram * grid_im], axis=0).astype(jnp.bfloat16)
        for part in chunks:
            c = lax.dot_general(h, g_re[:, part], NN, preferred_element_type=jnp.float32)
            s = lax.dot_general(h, g_im[:, part], NN, preferred_element_type=jnp.float32)
            z_re, z_im = c[:half] - s[half:], c[half:] + s[:half]
            for p in range(pairs):
                rows = pl.ds(p * NRAD, NRAD)
                a, b = t_re[rows, part], t_im[rows, part]
                zr, zi = z_re[p * NRAD : (p + 1) * NRAD], z_im[p * NRAD : (p + 1) * NRAD]
                image_ref[p : p + 1, part] = jnp.sum(a * zr - b * zi, axis=0, keepdims=True)
                image_ref[pairs + p : pairs + p + 1, part] = jnp.sum(a * zi + b * zr, axis=0, keepdims=True)

    def grid_norm(grid_re, grid_im):
        power = gram * (grid_re * grid_re + grid_im * grid_im)
        sums = [jnp.sum(power[p * NRAD : (p + 1) * NRAD], keepdims=True) for p in range(pairs)]
        return jnp.concatenate(sums, axis=0)

    def image_norm():
        power = jnp.sum(image_ref[...] * image_ref[...], axis=1, keepdims=True)
        return power[:pairs] + power[pairs:]

    def twice(column):
        return jnp.concatenate([column, column], axis=0)

    def per_row(column):
        return jnp.concatenate(
            [jnp.broadcast_to(column[p : p + 1], (NRAD, 1)) for p in range(pairs)], axis=0
        )

    grad_re, grad_im = adjoint(rhs_ref)
    norm = grid_norm(grad_re, grad_im)
    forward(grad_re, grad_im)
    step = norm / (image_norm() + EPS)
    res_ref[...] = rhs_ref[...] - twice(step) * image_ref[...]
    next_re, next_im = adjoint(res_ref)
    next_norm = grid_norm(next_re, next_im)
    momentum = per_row(next_norm / (norm + EPS))
    dir_re = next_re + momentum * grad_re
    dir_im = next_im + momentum * grad_im
    forward(dir_re, dir_im)
    last = next_norm / (image_norm() + EPS)
    res_ref[...] = res_ref[...] - twice(last) * image_ref[...]
    first_rows, last_rows = per_row(step), per_row(last)
    amp = jnp.concatenate(
        [first_rows * grad_re + last_rows * dir_re, first_rows * grad_im + last_rows * dir_im], axis=0
    ).astype(jnp.bfloat16)
    for part in mode_chunks:
        spread = lax.dot_general(amp, hot_ref[:, part], NN, preferred_element_type=jnp.float32)
        mask = radial == n_ref[:, part]
        rows = [
            jnp.sum(jnp.where(mask, spread[p * NRAD : (p + 1) * NRAD], 0.0), axis=0, keepdims=True)
            for p in range(2 * pairs)
        ]
        amp_ref[:, part] = jnp.concatenate(rows, axis=0).astype(amp_ref.dtype)


def solve(bins, az, ax, m, n, rhs, segs):
    pairs = rhs.shape[0] // 2
    mics, modes = rhs.shape[1], m.shape[1]
    vmem = pl.BlockSpec(memory_space=pltpu.VMEM)
    return pl.pallas_call(
        functools.partial(solve_kernel, pairs, segs, 512),
        out_shape=(
            jax.ShapeDtypeStruct((2 * pairs, modes), jnp.bfloat16),
            jax.ShapeDtypeStruct((2 * pairs, mics), jnp.float32),
        ),
        in_specs=[pl.BlockSpec(memory_space=pltpu.SMEM)] + [vmem] * 5,
        out_specs=(vmem, vmem),
        scratch_shapes=[
            pltpu.VMEM((pairs * NRAD, mics), jnp.float32),
            pltpu.VMEM((pairs * NRAD, mics), jnp.float32),
            pltpu.VMEM((ORDERS, mics), jnp.bfloat16),
            pltpu.VMEM((ORDERS, mics), jnp.bfloat16),
            pltpu.VMEM((2 * pairs, mics), jnp.float32),
            pltpu.VMEM((ORDERS, modes), jnp.bfloat16),
        ],
        compiler_params=pltpu.CompilerParams(vmem_limit_bytes=40 * 1024 * 1024),
    )(bins, az, ax, m, n, rhs)


def on_device(signal, mic_axial, mic_azimuth, mode_m, mode_n, freq_bins):
    seglen = signal.shape[2]
    segs = signal.shape[0]
    freqs = freq_bins.shape[0]
    own = freqs // lax.axis_size("mode")
    mic_code = lax.all_gather(mic_azimuth * AXIAL + mic_axial, "mic", axis=0, tiled=True)
    mode_code = lax.all_gather(
        (mode_m + ORDERS // 2) * NRAD + mode_n, "mode", axis=0, tiled=True
    )
    mics, modes = mic_code.shape[0], mode_code.shape[0]
    analysis = analysis_rows(freq_bins, seglen)
    spectra = lax.dot_general(
        analysis, signal, (((1,), (2,)), ((), ())), preferred_element_type=jnp.float32
    )
    spectra = spectra.reshape(freqs, 2, segs, signal.shape[1])
    rhs = lax.all_to_all(spectra, "mode", split_axis=0, concat_axis=3, tiled=True)
    rhs = rhs.transpose(1, 0, 2, 3).reshape(2 * own * segs, mics)
    bins = lax.dynamic_slice_in_dim(freq_bins, lax.axis_index("mode") * own, own)
    az = lax.shift_right_logical(mic_code, 6)[None, :]
    ax = jnp.bitwise_and(mic_code, AXIAL - 1)[None, :]
    m = (lax.shift_right_logical(mode_code, 5) - ORDERS // 2)[None, :]
    n = jnp.bitwise_and(mode_code, NRAD - 1)[None, :]
    amp, res = solve(bins, az, ax, m, n, rhs, segs)
    amp = amp.reshape(2, own, segs, modes)
    amp = lax.all_to_all(amp, "mode", split_axis=3, concat_axis=1, tiled=True)
    amp = lax.all_gather(amp, "mic", axis=2, tiled=True)
    res = lax.all_to_all(
        res.reshape(2, own, segs, mics), "mic", split_axis=3, concat_axis=2, tiled=True
    )
    weight = mics ** (-0.5) / jnp.sqrt(1.0 + mode_n.astype(jnp.float32))
    amplitude = amp.astype(jnp.float32).transpose(1, 0, 2, 3) * weight
    power = jnp.mean(jnp.sum(amplitude * amplitude, axis=1), axis=1)
    return (amplitude, power, res.transpose(1, 0, 2, 3))


def solution(mesh):
    in_specs = (P("mic", "mode", None), P("mic"), P("mic"), P("mode"), P("mode"), P())
    out_specs = (P(None, None, None, "mode"), P(None, "mode"), P("mode", None, None, "mic"))
    return jax.shard_map(
        on_device, mesh=mesh, in_specs=in_specs, out_specs=out_specs, check_vma=False
    )
```
